32 devices in a mesh: row: 4 (over y, x), col: 8 (over z, core).
Axes of the slice: x: 2, y: 2, z: 4, core: 2. Of those that a mesh axis runs over, the one named last changes fastest.
Arguments:
- matrix: float32 [4096, 4096], P('row', 'col'), may hold values from -8 to 48
- pivots: int32 [2, 128], replicated, may hold values from 256 to 4095, as said below
- lower_inverse: float32 [2, 128, 128], replicated, may hold values from -1 to 1, as said below
Outputs:
- factored: float32 [4096, 4096], P('row', 'col')
The draws below stay inside these ranges and needn't reach their ends.
Inputs may be any that keep to these rules, and one draw needn't show every extreme that they name: pivots[k, j] is the global row that panel k exchanges with global row k * 128 + j; all 256 entries are distinct. Each lower_inverse[k] is unit lower triangular.
All inputs are finite; a program needn't handle non-finite values.
Results may differ from the reference program's by a relative error of at most 0.0001.
Values sent between devices are 32-bit elements; how exact they have to be, the bound alone decides.
A program may use at most 64 MiB of HBM per device.

```python
import jax
import jax.numpy as jnp
from jax import lax

NB = 128
CB = 4
PANELS = 2
GRID_ROWS = 4
GRID_COLS = 8
RB = 8
ORDER = 4096


def pivot_table(key):
    inner_rows = jax.random.permutation(jax.random.fold_in(key, 11), ORDER - 2 * NB - 2).astype(jnp.int32) + 2 * NB + 1
    chosen = jnp.concatenate([inner_rows[:2 * NB - 2], jnp.array([2 * NB, ORDER - 1], dtype=jnp.int32)])
    shuffle = jax.random.permutation(jax.random.fold_in(key, 12), 2 * NB)
    return chosen[shuffle].reshape(PANELS, NB).astype(jnp.int32)


def draw_pivots(key, part):
    return pivot_table(key)


def draw_matrix(key, part):
    pivot_rows = pivot_table(key)
    grid_rows = ORDER // (RB * NB)
    grid_cols = ORDER // (CB * NB)
    target = jnp.full((ORDER,), -1, dtype=jnp.int32).at[pivot_rows.reshape(-1)].set(jnp.arange(PANELS * NB, dtype=jnp.int32))
    spots = jnp.arange(ORDER, dtype=jnp.int32)
    global_row = (spots % (RB * NB) // NB * grid_rows + spots // (RB * NB)) * NB + spots % NB
    global_col = (spots % (CB * NB) // NB * grid_cols + spots // (CB * NB)) * NB + spots % NB
    row_target = target[global_row]
    boost = jnp.where(global_col[None, :] == row_target[:, None], 40.0, 0.0).astype(jnp.float32)
    noise_key = jax.random.fold_in(key, 21)
    noise = jnp.clip(jax.random.normal(noise_key, (ORDER, ORDER), jnp.float32), -4.0, 4.0)
    return (noise + boost).astype(jnp.float32)


def draw_lower_inverse(key, part):
    values = jnp.clip(jax.random.normal(key, (PANELS, NB, NB), jnp.float32), -4.0, 4.0) * (0.5 * NB ** (-0.5))
    tri_rows = jnp.arange(NB)[:, None]
    tri_cols = jnp.arange(NB)[None, :]
    return jnp.where(tri_rows > tri_cols, values, jnp.where(tri_rows == tri_cols, 1.0, 0.0)).astype(jnp.float32)


def setup_inputs(seed: int = 0) -> dict:
    seeds = jax.random.split(jax.random.key(seed), 4)
    return {
        "matrix": draw_matrix(jax.random.fold_in(seeds[3], 71), 0),
        "pivots": draw_pivots(jax.random.fold_in(seeds[3], 71), 0),
        "lower_inverse": draw_lower_inverse(jax.random.fold_in(seeds[3], 71), 0),
    }


def reference(matrix, pivots, lower_inverse):
    global_mat = matrix.reshape(GRID_ROWS, RB, NB, GRID_COLS, CB, NB).transpose(1, 0, 2, 4, 3, 5).reshape(ORDER, ORDER)
    for panel_num in range(PANELS):
        first_row = panel_num * NB
        past_row = first_row + NB
        pivot_rows = pivots[panel_num]
        top_rows = global_mat[first_row:past_row]
        taken_rows = global_mat[pivot_rows]
        global_mat = global_mat.at[pivot_rows].set(top_rows).at[first_row:past_row].set(taken_rows)
        product = jnp.dot(lower_inverse[panel_num].astype(jnp.float32), global_mat[first_row:past_row, first_row:].astype(jnp.float32), precision=lax.Precision.HIGHEST, preferred_element_type=jnp.float32)
        diag_part = jnp.triu(product[:, :NB])
        global_mat = global_mat.at[first_row:past_row, first_row:past_row].set(diag_part)
        global_mat = global_mat.at[first_row:past_row, past_row:].set(product[:, NB:])
        panel_cols = global_mat[past_row:, first_row:past_row]
        lower_block = jax.scipy.linalg.solve_triangular(diag_part, panel_cols.T, trans=1, lower=False).T
        global_mat = global_mat.at[past_row:, first_row:past_row].set(lower_block)
        change = jnp.dot(lower_block.astype(jnp.float32), product[:, NB:].astype(jnp.float32), precision=lax.Precision.HIGHEST, preferred_element_type=jnp.float32)
        global_mat = global_mat.at[past_row:, past_row:].set(global_mat[past_row:, past_row:] - change)
    return global_mat.reshape(RB, GRID_ROWS, NB, CB, GRID_COLS, NB).transpose(1, 0, 2, 4, 3, 5).reshape(ORDER, ORDER)
```

```python
import functools

import jax
import jax.numpy as jnp
from jax import lax
from jax.experimental import pallas as pl
from jax.experimental.pallas import tpu as pltpu
from jax.sharding import PartitionSpec as P

MESH = pl.DeviceIdType.MESH
F32 = jnp.float32
BF16 = jnp.bfloat16
CHUNKS = 8
TILES = 4


def mm(left, right):
    return jnp.dot(left, right, preferred_element_type=F32)


def exact(left, right):
    return jnp.dot(left, right, precision=lax.Precision.HIGHEST, preferred_element_type=F32)


def halves(value):
    high = value.astype(BF16)
    return high, (value - high.astype(F32)).astype(BF16)


def thirds(value):
    high = value.astype(BF16)
    rest = value - high.astype(F32)
    middle = rest.astype(BF16)
    return high, middle, (rest - middle.astype(F32)).astype(BF16)


def select(chosen, value):
    high, middle, low = thirds(value)
    return mm(chosen, high) + (mm(chosen, middle) + mm(chosen, low))


def dot3(left, right):
    left_high, left_low = left
    right_high, right_low = right
    return mm(left_high, right_high) + (mm(left_low, right_high) + mm(left_high, right_low))


def upper_inverse(upper, rows, cols):
    on_diag = rows == cols
    eye = jnp.where(on_diag, 1.0, 0.0)
    kept = jnp.where(on_diag, upper, 0.0)
    scaled = upper / jnp.sum(kept, axis=1, keepdims=True)
    power = jnp.where(rows < cols, -scaled, 0.0)
    result = eye + power
    reach = 2
    while reach < upper.shape[0]:
        power = exact(power, power)
        result = result + exact(result, power)
        reach = reach * 2
    return result / jnp.sum(kept, axis=0, keepdims=True)


def kernel(R, C, nb, a_hbm, piv_ref, linv_ref, out_hbm,
           a_v, asw, sel, sel_t, pm, pf, rsbuf, tops, tp, dpart, dbuf, dh, pan, res,
           u_hi, u_lo, u_f, hit,
           load_sem, out_sem, d_s, d_r, tp_s, tp_r, dh_s, dh_r, rs_s, rs_r, ag_s, ag_r,
           to_s, to_r, ch_s, ch_r, sb_s, sb_r, re_s, re_r):
    height, width = a_v.shape
    two = 2 * nb
    ch = two // R
    ck = height // CHUNKS
    r = lax.axis_index("row")
    c = lax.axis_index("col")
    s = lax.rem(c, 2)
    sibling = {"col": c + 1 - 2 * s}
    half = C // 2

    load = pltpu.make_async_copy(a_hbm, a_v, load_sem)
    load.start()

    barrier = pltpu.get_barrier_semaphore()
    for off in range(1, R):
        pl.semaphore_signal(barrier, inc=1, device_id={"row": lax.rem(r + off, R)}, device_id_type=MESH)
    for off in range(1, half):
        pl.semaphore_signal(barrier, inc=1, device_id={"col": lax.rem(c + 2 * off, C)}, device_id_type=MESH)
    pl.semaphore_signal(barrier, inc=1, device_id=sibling, device_id_type=MESH)

    shift = nb.bit_length() - 1
    rshift = R.bit_length() - 1
    lane = lax.broadcasted_iota(jnp.int32, (nb, nb), 1)
    sub = lax.broadcasted_iota(jnp.int32, (nb, nb), 0)
    for k in range(2):
        p = piv_ref[k:k + 1, :]
        block = jnp.right_shift(p, shift)
        local = jnp.left_shift(jnp.right_shift(block, rshift), shift) + jnp.bitwise_and(p, nb - 1)
        local = jnp.where(jnp.bitwise_and(block, R - 1) == r, local, -1)
        wide = jnp.broadcast_to(local, (nb, nb))
        tall = wide.astype(F32).T
        for t in range(height // nb):
            spots = slice(t * nb, (t + 1) * nb)
            sel[spots, k * nb:(k + 1) * nb] = jnp.where(wide == sub + t * nb, 1.0, 0.0).astype(BF16)
            sel_t[k * nb:(k + 1) * nb, spots] = jnp.where(
                tall == (lane + t * nb).astype(F32), 1.0, 0.0).astype(BF16)

    load.wait()
    pl.semaphore_wait(barrier, R - 1 + half - 1 + 1)

    def remote(src, dst, send, recv, where):
        return pltpu.make_async_remote_copy(
            src_ref=src, dst_ref=dst, send_sem=send, recv_sem=recv, device_id=where, device_id_type=MESH)

    def row_peer(off):
        return {"row": lax.rem(r + off, R)}

    def tp_copy(off):
        q = jnp.minimum(r, 1)
        return remote(a_v.at[0:nb, 0:nb], tp.at[pl.ds(pl.multiple_of(q * nb, nb), nb)],
                      tp_s.at[off - 1], tp_r.at[q], row_peer(off))

    def tops_copy(off):
        q = jnp.minimum(r, 1)
        return remote(a_v.at[0:nb], tops.at[pl.ds(pl.multiple_of(q * nb, nb), nb)],
                      to_s.at[off - 1], to_r.at[q], row_peer(off))

    def d_copy(off):
        return remote(dpart, dbuf.at[off - 1], d_s.at[off - 1], d_r.at[off - 1], row_peer(off))

    def rs_copy(off):
        to = lax.rem(r + off, R)
        return remote(pm.at[pl.ds(pl.multiple_of(to * ch, ch), ch)], rsbuf.at[off - 1],
                      rs_s.at[off - 1], rs_r.at[off - 1], {"row": to})

    def ag_copy(off):
        mine = pf.at[pl.ds(pl.multiple_of(r * ch, ch), ch)]
        return remote(mine, mine, ag_s.at[off - 1], ag_r.at[off - 1], row_peer(off))

    def ag_in(off):
        src = lax.rem(r - off + R, R)
        there = pf.at[pl.ds(pl.multiple_of(src * ch, ch), ch)]
        return remote(there, there, ag_s.at[off - 1], ag_r.at[off - 1], row_peer(off))

    def chain_copy(k):
        part = pan.at[s, pl.ds(k * ck, ck)]
        return remote(part, part, ch_s.at[k], ch_r.at[k], {"col": jnp.minimum(c + 2, C - 2 + s)})

    def sib_copy(k):
        part = pan.at[s, pl.ds(k * ck, ck)]
        return remote(part, part, sb_s.at[k], sb_r.at[k], sibling)

    def sib_in(k):
        part = pan.at[1 - s, pl.ds(k * ck, ck)]
        return remote(part, part, sb_s.at[k], sb_r.at[k], sibling)

    def dh_copy():
        return remote(dh.at[s], dh.at[s], dh_s, dh_r, sibling)

    def dh_in():
        return remote(dh.at[1 - s], dh.at[1 - s], dh_s, dh_r, sibling)

    def res_copy(j, off):
        part = res.at[2 * j:2 * j + 2]
        return remote(part, part, re_s.at[j, off - 1], re_r.at[j], {"col": lax.rem(c + 2 * off, C)})

    is_top = r < 2
    at_root = c < 2

    @pl.when(at_root)
    def _():
        dpart[...] = select(sel_t[...], a_v[:, 0:nb])
        for off in range(1, R):
            d_copy(off).start()

        @pl.when(is_top)
        def _():
            for off in range(1, R):
                tp_copy(off).start()
            tp[pl.ds(pl.multiple_of(jnp.minimum(r, 1) * nb, nb), nb), :] = a_v[0:nb, 0:nb]

    @pl.loop(0, width // nb)
    def _(t):
        spots = pl.ds(pl.multiple_of(t * nb, nb), nb)
        pm[:, spots] = select(sel_t[...], a_v[:, spots])

    for off in range(1, R):
        rs_copy(off).start()

    @pl.when(is_top)
    def _():
        for off in range(1, R):
            tops_copy(off).start()
        tops[pl.ds(pl.multiple_of(jnp.minimum(r, 1) * nb, nb), nb), :] = a_v[0:nb, :]

    ones = jnp.full((two, nb), 1.0, BF16)

    @pl.loop(0, TILES)
    def _(t):
        spots = pl.ds(pl.multiple_of(t * (height // TILES), height // TILES), height // TILES)
        hit[spots, :] = mm(sel[spots, :], ones)

    @pl.when(at_root)
    def _():
        for q in range(2):
            @pl.when(r != q)
            def _():
                part = tp.at[q * nb:(q + 1) * nb]
                remote(part, part, tp_s.at[0], tp_r.at[q], row_peer(1)).wait_recv()
        high, middle, low = thirds(tp[...])
        for k in range(CHUNKS):
            spots = slice(k * ck, (k + 1) * ck)
            chosen = sel[spots, :]
            placed = mm(chosen, high) + (mm(chosen, middle) + mm(chosen, low))
            pan[s, spots, :] = jnp.where(hit[spots, :] > 0.5, placed, a_v[spots, 0:nb])
            chain_copy(k).start()
            sib_copy(k).start()

    @pl.when(at_root)
    def _():
        total = dpart[...]
        for off in range(1, R):
            d_copy(off).wait_recv()
            total = total + dbuf[off - 1]
        dh[s] = total
        dh_copy().start()

    def forward(k):
        @pl.when(c >= 2)
        def _():
            chain_copy(k).wait_recv()

            @pl.when(c + 2 < C)
            def _():
                chain_copy(k).start()
            sib_copy(k).start()

    forward(0)

    own = pl.ds(pl.multiple_of(r * ch, ch), ch)
    total = pm[own, :]
    for off in range(1, R):
        rs_copy(off).wait_recv()
        total = total + rsbuf[off - 1]
    pf[own, :] = total
    for off in range(1, R):
        ag_copy(off).start()

    @pl.when(at_root)
    def _():
        dh_in().wait_recv()
        upper00 = jnp.where(sub <= lane, exact(linv_ref[0], dh[0, 0:nb, :]), 0.0)
        inv0 = upper_inverse(upper00, sub, lane)
        low10 = exact(dh[0, nb:two, :], inv0)
        res[0] = inv0
        res[1] = low10
        for off in range(1, half):
            res_copy(0, off).start()
        upper01 = exact(linv_ref[0], dh[1, 0:nb, :])
        rest = dh[1, nb:two, :] - exact(low10, upper01)
        upper11 = jnp.where(sub <= lane, exact(linv_ref[1], rest), 0.0)
        cross = exact(inv0, upper01)
        inv1 = upper_inverse(upper11, sub, lane)
        res[2] = -exact(cross, inv1)
        res[3] = inv1
        for off in range(1, half):
            res_copy(1, off).start()

    for k in range(1, CHUNKS):
        forward(k)

    for q in range(2):
        @pl.when(r != q)
        def _():
            part = tops.at[q * nb:(q + 1) * nb]
            remote(part, part, to_s.at[0], to_r.at[q], row_peer(1)).wait_recv()

    @pl.loop(0, width // nb)
    def _(t):
        spots = pl.ds(pl.multiple_of(t * nb, nb), nb)
        placed = select(sel[...], tops[:, spots])
        asw[:, spots] = jnp.where(hit[...] > 0.5, placed, a_v[:, spots])

    for off in range(1, R):
        ag_in(off).wait_recv()

    @pl.when(c >= 2)
    def _():
        res_copy(0, 1).wait_recv()
    inv_low0 = linv_ref[0]
    inv_low1 = linv_ref[1]
    mixed = -exact(exact(inv_low1, res[1]), inv_low0)
    u_f[0:nb, :] = dot3(halves(inv_low0), halves(pf[0:nb, :]))
    u_f[nb:two, :] = (dot3(halves(mixed), halves(pf[0:nb, :]))
                      + dot3(halves(inv_low1), halves(pf[nb:two, :])))
    high, low = halves(u_f[...])
    u_hi[...] = high
    u_lo[...] = low

    for k in range(CHUNKS):
        sib_in(k).wait_recv()

    @pl.when(c >= 2)
    def _():
        res_copy(1, 1).wait_recv()

    step = height // TILES
    inv0 = halves(res[0])
    cross = halves(res[2])
    inv1 = halves(res[3])

    def update(t, start):
        spots = pl.ds(start, step)
        left0 = halves(pan[0, spots, :])
        left1 = halves(pan[1, spots, :])
        low0 = dot3(left0, inv0)
        low1 = dot3(left0, cross) + dot3(left1, inv1)
        high, low = halves(jnp.concatenate([low0, low1], axis=1))
        asw[spots, :] = asw[spots, :] - dot3((high, low), (u_hi[...], u_lo[...]))

        @pl.when(c == 0)
        def _():
            asw[spots, 0:nb] = low0

        @pl.when(c == 1)
        def _():
            asw[spots, 0:nb] = low1

    def store(t):
        part = pl.ds(t * step, step)
        return pltpu.make_async_copy(asw.at[part], out_hbm.at[part], out_sem.at[t])

    for t in range(TILES):
        update(t, t * step)
        if t == 0:
            @pl.when(r == 0)
            def _():
                asw[0:nb, :] = u_f[0:nb, :]

                @pl.when(c == 0)
                def _():
                    asw[0:nb, 0:nb] = jnp.where(sub <= lane, u_f[0:nb, 0:nb], 0.0)

            @pl.when(r == 1)
            def _():
                asw[0:nb, :] = u_f[nb:two, :]

                @pl.when(c == 0)
                def _():
                    asw[0:nb, 0:nb] = res[1]

                @pl.when(c == 1)
                def _():
                    asw[0:nb, 0:nb] = jnp.where(sub <= lane, u_f[nb:two, 0:nb], 0.0)
        store(t).start()

    for off in range(1, R):
        rs_copy(off).wait_send()
        ag_copy(off).wait_send()

    @pl.when(is_top)
    def _():
        for off in range(1, R):
            tops_copy(off).wait_send()

        @pl.when(at_root)
        def _():
            for off in range(1, R):
                tp_copy(off).wait_send()

    for k in range(CHUNKS):
        sib_copy(k).wait_send()

        @pl.when(c + 2 < C)
        def _():
            chain_copy(k).wait_send()

    @pl.when(at_root)
    def _():
        dh_copy().wait_send()
        for off in range(1, R):
            d_copy(off).wait_send()
        for off in range(1, half):
            res_copy(0, off).wait_send()
            res_copy(1, off).wait_send()
    for t in range(TILES):
        store(t).wait()


def on_device(matrix, pivots, lower_inverse):
    R = lax.axis_size("row")
    C = lax.axis_size("col")
    height, width = matrix.shape
    nb = lower_inverse.shape[1]
    two = 2 * nb
    dma = pltpu.SemaphoreType.DMA
    vm = pltpu.VMEM
    return pl.pallas_call(
        functools.partial(kernel, R, C, nb),
        out_shape=jax.ShapeDtypeStruct((height, width), F32),
        in_specs=[pl.BlockSpec(memory_space=pl.ANY), pl.BlockSpec(memory_space=pltpu.VMEM),
                  pl.BlockSpec(memory_space=pltpu.VMEM)],
        out_specs=pl.BlockSpec(memory_space=pl.ANY),
        scratch_shapes=[
            vm((height, width), F32), vm((height, width), F32),
            vm((height, two), BF16), vm((two, height), BF16),
            vm((two, width), F32), vm((two, width), F32),
            vm((R - 1, two // R, width), F32), vm((two, width), F32),
            vm((two, nb), F32), vm((two, nb), F32), vm((R - 1, two, nb), F32),
            vm((2, two, nb), F32), vm((2, height, nb), F32), vm((4, nb, nb), F32),
            vm((two, width), BF16), vm((two, width), BF16), vm((two, width), F32),
            vm((height, nb), F32),
            dma, dma((TILES,)), dma((R - 1,)), dma((R - 1,)), dma((R - 1,)), dma((2,)), dma, dma,
            dma((R - 1,)), dma((R - 1,)), dma((R - 1,)), dma((R - 1,)),
            dma((R - 1,)), dma((2,)), dma((CHUNKS,)), dma((CHUNKS,)), dma((CHUNKS,)), dma((CHUNKS,)),
            dma((2, C // 2 - 1)), dma((2,)),
        ],
        compiler_params=pltpu.CompilerParams(
            collective_id=0, has_side_effects=True, vmem_limit_bytes=40 * 1024 * 1024),
    )(matrix, pivots, lower_inverse)


def solution(mesh):
    return jax.shard_map(
        on_device,
        mesh=mesh,
        in_specs=(P("row", "col"), P(), P()),
        out_specs=P("row", "col"),
        check_vma=False,
    )
```

```python
import functools

import jax
import jax.numpy as jnp
from jax import lax
from jax.experimental import pallas as pl
from jax.experimental.pallas import tpu as pltpu
from jax.sharding import PartitionSpec as P

MESH = pl.DeviceIdType.MESH
F32 = jnp.float32
BF16 = jnp.bfloat16
CHUNKS = 8
EARLY = 2
TILES = 4


def mm(left, right):
    return jnp.dot(left, right, preferred_element_type=F32)


def exact(left, right):
    return jnp.dot(left, right, precision=lax.Precision.HIGHEST, preferred_element_type=F32)


def halves(value):
    high = value.astype(BF16)
    return high, (value - high.astype(F32)).astype(BF16)


def thirds(value):
    high = value.astype(BF16)
    rest = value - high.astype(F32)
    middle = rest.astype(BF16)
    return high, middle, (rest - middle.astype(F32)).astype(BF16)


def select(chosen, value):
    high, middle, low = thirds(value)
    return mm(chosen, high) + (mm(chosen, middle) + mm(chosen, low))


def dot3(left, right):
    left_high, left_low = left
    right_high, right_low = right
    return mm(left_high, right_high) + (mm(left_low, right_high) + mm(left_high, right_low))


def upper_inverse(upper, rows, cols):
    on_diag = rows == cols
    eye = jnp.where(on_diag, 1.0, 0.0)
    kept = jnp.where(on_diag, upper, 0.0)
    scaled = upper / jnp.sum(kept, axis=1, keepdims=True)
    power = jnp.where(rows < cols, -scaled, 0.0)
    result = eye + power
    reach = 2
    while reach < upper.shape[0]:
        power = exact(power, power)
        result = result + exact(result, power)
        reach = reach * 2
    return result / jnp.sum(kept, axis=0, keepdims=True)


def kernel(R, C, nb, a_hbm, piv_hbm, linv_hbm, asw,
           a_v, piv_ref, linv_ref, sel, sel_t, pm, pf, rsbuf, tops, tp, dpart, dbuf, dh, pan, res,
           u_hi, u_lo, u_f, hit,
           load_sem, piv_sem, linv_sem, d_s, d_r, tp_s, tp_r, rs_s, rs_r, ag_s, ag_r,
           to_s, to_r, ch_s, ch_r, sb_s, sb_r):
    height, width = a_v.shape
    two = 2 * nb
    ch = two // R
    ck = height // CHUNKS
    r = lax.axis_index("row")
    c = lax.axis_index("col")
    s = lax.rem(c, 2)
    sibling = {"col": c + 1 - 2 * s}

    load = pltpu.make_async_copy(a_hbm, a_v, load_sem)
    load_piv = pltpu.make_async_copy(piv_hbm, piv_ref, piv_sem)
    load_linv = pltpu.make_async_copy(linv_hbm, linv_ref, linv_sem)
    load_piv.start()
    load.start()
    load_linv.start()

    barrier = pltpu.get_barrier_semaphore()
    for off in range(1, R):
        pl.semaphore_signal(barrier, inc=1, device_id={"row": lax.rem(r + off, R)}, device_id_type=MESH)
    has_after = c + 2 < C
    has_before = c >= 2

    @pl.when(has_after)
    def _():
        pl.semaphore_signal(barrier, inc=1, device_id={"col": jnp.minimum(c + 2, C - 1)}, device_id_type=MESH)

    @pl.when(has_before)
    def _():
        pl.semaphore_signal(barrier, inc=1, device_id={"col": jnp.maximum(c - 2, 0)}, device_id_type=MESH)

    pl.semaphore_signal(barrier, inc=1, device_id=sibling, device_id_type=MESH)

    load_piv.wait()
    shift = nb.bit_length() - 1
    rshift = R.bit_length() - 1
    lane = lax.broadcasted_iota(jnp.int32, (nb, nb), 1)
    sub = lax.broadcasted_iota(jnp.int32, (nb, nb), 0)
    for k in range(2):
        p = piv_ref[k:k + 1, :]
        block = jnp.right_shift(p, shift)
        local = jnp.left_shift(jnp.right_shift(block, rshift), shift) + jnp.bitwise_and(p, nb - 1)
        local = jnp.where(jnp.bitwise_and(block, R - 1) == r, local, -1)
        wide = jnp.broadcast_to(local, (nb, nb))
        tall = wide.astype(F32).T
        for t in range(height // nb):
            spots = slice(t * nb, (t + 1) * nb)
            sel[spots, k * nb:(k + 1) * nb] = jnp.where(wide == sub + t * nb, 1.0, 0.0).astype(BF16)
            sel_t[k * nb:(k + 1) * nb, spots] = jnp.where(
                tall == (lane + t * nb).astype(F32), 1.0, 0.0).astype(BF16)

    load.wait()
    load_linv.wait()
    pl.semaphore_wait(barrier, R + jnp.minimum(c // 2, 1) + jnp.minimum((C - 1 - c) // 2, 1))

    def remote(src, dst, send, recv, where):
        return pltpu.make_async_remote_copy(
            src_ref=src, dst_ref=dst, send_sem=send, recv_sem=recv, device_id=where, device_id_type=MESH)

    def row_peer(off):
        return {"row": lax.rem(r + off, R)}

    def tp_copy(off):
        q = jnp.minimum(r, 1)
        return remote(a_v.at[0:nb, 0:nb], tp.at[pl.ds(pl.multiple_of(q * nb, nb), nb)],
                      tp_s.at[off - 1], tp_r.at[q], row_peer(off))

    def tops_copy(off):
        q = jnp.minimum(r, 1)
        return remote(a_v.at[0:nb], tops.at[pl.ds(pl.multiple_of(q * nb, nb), nb)],
                      to_s.at[off - 1], to_r.at[q], row_peer(off))

    def d_copy(off):
        return remote(dpart, dbuf.at[off - 1], d_s.at[off - 1], d_r.at[off - 1], row_peer(off))

    def rs_copy(off):
        to = lax.rem(r + off, R)
        return remote(pm.at[pl.ds(pl.multiple_of(to * ch, ch), ch)], rsbuf.at[off - 1],
                      rs_s.at[off - 1], rs_r.at[off - 1], {"row": to})

    def ag_copy(off):
        mine = pf.at[pl.ds(pl.multiple_of(r * ch, ch), ch)]
        return remote(mine, mine, ag_s.at[off - 1], ag_r.at[off - 1], row_peer(off))

    def ag_in(off):
        src = lax.rem(r - off + R, R)
        there = pf.at[pl.ds(pl.multiple_of(src * ch, ch), ch)]
        return remote(there, there, ag_s.at[off - 1], ag_r.at[off - 1], row_peer(off))

    def piece(side, k):
        if k < CHUNKS:
            return pan.at[side, pl.ds(k * ck, ck)]
        return dh.at[side, pl.ds((k - CHUNKS) * nb, nb)]

    def chain_copy(k):
        part = piece(s, k)
        return remote(part, part, ch_s.at[k], ch_r.at[k], {"col": jnp.minimum(c + 2, C - 2 + s)})

    def sib_copy(k):
        part = piece(s, k)
        return remote(part, part, sb_s.at[k], sb_r.at[k], sibling)

    def sib_in(k):
        part = piece(1 - s, k)
        return remote(part, part, sb_s.at[k], sb_r.at[k], sibling)

    is_top = r < 2
    at_root = c < 2

    @pl.when(at_root)
    def _():
        dpart[...] = select(sel_t[...], a_v[:, 0:nb])
        for off in range(1, R):
            d_copy(off).start()

        @pl.when(is_top)
        def _():
            for off in range(1, R):
                tp_copy(off).start()
            tp[pl.ds(pl.multiple_of(jnp.minimum(r, 1) * nb, nb), nb), :] = a_v[0:nb, 0:nb]

    ones = jnp.full((two, nb), 1.0, BF16)

    @pl.loop(0, TILES)
    def _(t):
        spots = pl.ds(pl.multiple_of(t * (height // TILES), height // TILES), height // TILES)
        hit[spots, :] = mm(sel[spots, :], ones)

    def panel(first, last):
        high, middle, low = thirds(tp[...])
        for k in range(first, last):
            spots = slice(k * ck, (k + 1) * ck)
            chosen = sel[spots, :]
            placed = mm(chosen, high) + (mm(chosen, middle) + mm(chosen, low))
            pan[s, spots, :] = jnp.where(hit[spots, :] > 0.5, placed, a_v[spots, 0:nb])
            chain_copy(k).start()
            sib_copy(k).start()

    @pl.when(at_root)
    def _():
        for q in range(2):
            @pl.when(r != q)
            def _():
                part = tp.at[q * nb:(q + 1) * nb]
                remote(part, part, tp_s.at[0], tp_r.at[q], row_peer(1)).wait_recv()
        panel(0, EARLY)

    @pl.loop(0, width // nb)
    def _(t):
        spots = pl.ds(pl.multiple_of(t * nb, nb), nb)
        pm[:, spots] = select(sel_t[...], a_v[:, spots])

    for off in range(1, R):
        rs_copy(off).start()

    @pl.when(is_top)
    def _():
        for off in range(1, R):
            tops_copy(off).start()
        tops[pl.ds(pl.multiple_of(jnp.minimum(r, 1) * nb, nb), nb), :] = a_v[0:nb, :]

    @pl.when(at_root)
    def _():
        total = dpart[...]
        for off in range(1, R):
            d_copy(off).wait_recv()
            total = total + dbuf[off - 1]
        dh[s] = total
        for k in range(CHUNKS, CHUNKS + 2):
            chain_copy(k).start()
            sib_copy(k).start()
        panel(EARLY, CHUNKS)

    def forward(k):
        @pl.when(c >= 2)
        def _():
            chain_copy(k).wait_recv()

            @pl.when(c + 2 < C)
            def _():
                chain_copy(k).start()
            sib_copy(k).start()

    for k in range(EARLY):
        forward(k)
    forward(CHUNKS)
    forward(CHUNKS + 1)

    own = pl.ds(pl.multiple_of(r * ch, ch), ch)
    total = pm[own, :]
    for off in range(1, R):
        rs_copy(off).wait_recv()
        total = total + rsbuf[off - 1]
    pf[own, :] = total
    for off in range(1, R):
        ag_copy(off).start()

    left = list(range(EARLY, CHUNKS))

    def some(count):
        for _ in range(min(count, len(left))):
            forward(left.pop(0))

    sib_in(CHUNKS).wait_recv()
    sib_in(CHUNKS + 1).wait_recv()
    upper00 = jnp.where(sub <= lane, exact(linv_ref[0], dh[0, 0:nb, :]), 0.0)
    res[0] = upper_inverse(upper00, sub, lane)
    some(2)
    res[1] = exact(dh[0, nb:two, :], res[0])
    upper01 = exact(linv_ref[0], dh[1, 0:nb, :])
    rest = dh[1, nb:two, :] - exact(res[1], upper01)
    upper11 = jnp.where(sub <= lane, exact(linv_ref[1], rest), 0.0)
    res[2] = -exact(res[0], upper01)
    some(2)
    res[3] = upper_inverse(upper11, sub, lane)
    some(1)
    res[2] = exact(res[2], res[3])
    mixed = -exact(exact(linv_ref[1], res[1]), linv_ref[0])
    some(CHUNKS)

    for q in range(2):
        @pl.when(r != q)
        def _():
            part = tops.at[q * nb:(q + 1) * nb]
            remote(part, part, to_s.at[0], to_r.at[q], row_peer(1)).wait_recv()

    @pl.loop(0, width // nb)
    def _(t):
        spots = pl.ds(pl.multiple_of(t * nb, nb), nb)
        placed = select(sel[...], tops[:, spots])
        asw[:, spots] = jnp.where(hit[...] > 0.5, placed, a_v[:, spots])

    for off in range(1, R):
        ag_in(off).wait_recv()

    inv_low0 = linv_ref[0]
    inv_low1 = linv_ref[1]
    u_f[0:nb, :] = dot3(halves(inv_low0), halves(pf[0:nb, :]))
    u_f[nb:two, :] = (dot3(halves(mixed), halves(pf[0:nb, :]))
                      + dot3(halves(inv_low1), halves(pf[nb:two, :])))
    high, low = halves(u_f[...])
    u_hi[...] = high
    u_lo[...] = low

    for k in range(CHUNKS):
        sib_in(k).wait_recv()

    step = height // TILES
    inv0 = halves(res[0])
    cross = halves(res[2])
    inv1 = halves(res[3])

    def update(t, start):
        spots = pl.ds(start, step)
        left0 = halves(pan[0, spots, :])
        left1 = halves(pan[1, spots, :])
        low0 = dot3(left0, inv0)
        low1 = dot3(left0, cross) + dot3(left1, inv1)
        high, low = halves(jnp.concatenate([low0, low1], axis=1))
        asw[spots, :] = asw[spots, :] - dot3((high, low), (u_hi[...], u_lo[...]))

        @pl.when(c == 0)
        def _():
            asw[spots, 0:nb] = low0

        @pl.when(c == 1)
        def _():
            asw[spots, 0:nb] = low1

    for t in range(TILES):
        update(t, t * step)
        if t == 0:
            @pl.when(r == 0)
            def _():
                asw[0:nb, :] = u_f[0:nb, :]

                @pl.when(c == 0)
                def _():
                    asw[0:nb, 0:nb] = jnp.where(sub <= lane, u_f[0:nb, 0:nb], 0.0)

            @pl.when(r == 1)
            def _():
                asw[0:nb, :] = u_f[nb:two, :]

                @pl.when(c == 0)
                def _():
                    asw[0:nb, 0:nb] = res[1]

                @pl.when(c == 1)
                def _():
                    asw[0:nb, 0:nb] = jnp.where(sub <= lane, u_f[nb:two, 0:nb], 0.0)

    for off in range(1, R):
        rs_copy(off).wait_send()
        ag_copy(off).wait_send()

    @pl.when(is_top)
    def _():
        for off in range(1, R):
            tops_copy(off).wait_send()

        @pl.when(at_root)
        def _():
            for off in range(1, R):
                tp_copy(off).wait_send()

    for k in range(CHUNKS + 2):
        sib_copy(k).wait_send()

        @pl.when(c + 2 < C)
        def _():
            chain_copy(k).wait_send()

    @pl.when(at_root)
    def _():
        for off in range(1, R):
            d_copy(off).wait_send()


def on_device(matrix, pivots, lower_inverse):
    R = lax.axis_size("row")
    C = lax.axis_size("col")
    height, width = matrix.shape
    nb = lower_inverse.shape[1]
    two = 2 * nb
    dma = pltpu.SemaphoreType.DMA
    vm = pltpu.VMEM
    return pl.pallas_call(
        functools.partial(kernel, R, C, nb),
        out_shape=jax.ShapeDtypeStruct((height, width), F32),
        in_specs=[pl.BlockSpec(memory_space=pl.ANY)] * 3,
        out_specs=pl.BlockSpec(memory_space=pltpu.VMEM),
        scratch_shapes=[
            vm((height, width), F32), vm((2, nb), jnp.int32), vm((2, nb, nb), F32),
            vm((height, two), BF16), vm((two, height), BF16),
            vm((two, width), F32), vm((two, width), F32),
            vm((R - 1, two // R, width), F32), vm((two, width), F32),
            vm((two, nb), F32), vm((two, nb), F32), vm((R - 1, two, nb), F32),
            vm((2, two, nb), F32), vm((2, height, nb), F32), vm((4, nb, nb), F32),
            vm((two, width), BF16), vm((two, width), BF16), vm((two, width), F32),
            vm((height, nb), F32),
            dma, dma, dma, dma((R - 1,)), dma((R - 1,)), dma((R - 1,)), dma((2,)),
            dma((R - 1,)), dma((R - 1,)), dma((R - 1,)), dma((R - 1,)),
            dma((R - 1,)), dma((2,)), dma((CHUNKS + 2,)), dma((CHUNKS + 2,)),
            dma((CHUNKS + 2,)), dma((CHUNKS + 2,)),
        ],
        compiler_params=pltpu.CompilerParams(
            collective_id=0, has_side_effects=True, vmem_limit_bytes=61 * 1024 * 1024),
    )(matrix, pivots, lower_inverse)


def solution(mesh):
    return jax.shard_map(
        on_device,
        mesh=mesh,
        in_specs=(P("row", "col"), P(), P()),
        out_specs=P("row", "col"),
        check_vma=False,
    )
```

```python
import functools

import jax
import jax.numpy as jnp
from jax import lax
from jax.experimental import pallas as pl
from jax.experimental.pallas import tpu as pltpu
from jax.sharding import PartitionSpec as P

MESH = pl.DeviceIdType.MESH
F32 = jnp.float32
BF16 = jnp.bfloat16
CHUNKS = 16
EARLY = 3
TILES = 4


def mm(left, right):
    return jnp.dot(left, right, preferred_element_type=F32)


def exact(left, right):
    return jnp.dot(left, right, precision=lax.Precision.HIGHEST, preferred_element_type=F32)


def halves(value):
    high = value.astype(BF16)
    return high, (value - high.astype(F32)).astype(BF16)


def thirds(value):
    high = value.astype(BF16)
    rest = value - high.astype(F32)
    middle = rest.astype(BF16)
    return high, middle, (rest - middle.astype(F32)).astype(BF16)


def select(chosen, value):
    high, middle, low = thirds(value)
    return mm(chosen, high) + (mm(chosen, middle) + mm(chosen, low))


def dot3(left, right):
    left_high, left_low = left
    right_high, right_low = right
    return mm(left_high, right_high) + (mm(left_low, right_high) + mm(left_high, right_low))


def upper_inverse(upper, rows, cols):
    on_diag = rows == cols
    eye = jnp.where(on_diag, 1.0, 0.0)
    kept = jnp.where(on_diag, upper, 0.0)
    scaled = upper / jnp.sum(kept, axis=1, keepdims=True)
    power = jnp.where(rows < cols, -scaled, 0.0)
    result = eye + power
    reach = 2
    while reach < upper.shape[0]:
        power = exact(power, power)
        result = result + exact(result, power)
        reach = reach * 2
    return result / jnp.sum(kept, axis=0, keepdims=True)


def kernel(R, C, nb, a_hbm, piv_hbm, linv_hbm, asw,
           a_v, piv_ref, linv_ref, sel, sel_t, pm, pf, rsbuf, tops, tp, dpart, dbuf, dh, pan, res,
           u_hi, u_lo, u_f, hit,
           load_sem, piv_sem, linv_sem, d_s, d_r, tp_s, tp_r, rs_s, rs_r, ag_s, ag_r,
           to_s, to_r, ch_s, ch_r, sb_s, sb_r):
    height, width = a_v.shape
    two = 2 * nb
    ch = two // R
    ck = height // CHUNKS
    r = lax.axis_index("row")
    c = lax.axis_index("col")
    s = lax.rem(c, 2)
    sibling = {"col": c + 1 - 2 * s}

    load = pltpu.make_async_copy(a_hbm, a_v, load_sem)
    load_piv = pltpu.make_async_copy(piv_hbm, piv_ref, piv_sem)
    load_linv = pltpu.make_async_copy(linv_hbm, linv_ref, linv_sem)
    load_piv.start()
    load.start()
    load_linv.start()

    barrier = pltpu.get_barrier_semaphore()
    for off in range(1, R):
        pl.semaphore_signal(barrier, inc=1, device_id={"row": lax.rem(r + off, R)}, device_id_type=MESH)
    has_after = c + 2 < C
    has_before = c >= 2

    @pl.when(has_after)
    def _():
        pl.semaphore_signal(barrier, inc=1, device_id={"col": jnp.minimum(c + 2, C - 1)}, device_id_type=MESH)

    @pl.when(has_before)
    def _():
        pl.semaphore_signal(barrier, inc=1, device_id={"col": jnp.maximum(c - 2, 0)}, device_id_type=MESH)

    pl.semaphore_signal(barrier, inc=1, device_id=sibling, device_id_type=MESH)

    load_piv.wait()
    shift = nb.bit_length() - 1
    rshift = R.bit_length() - 1
    lane = lax.broadcasted_iota(jnp.int32, (nb, nb), 1)
    sub = lax.broadcasted_iota(jnp.int32, (nb, nb), 0)
    for k in range(2):
        p = piv_ref[k:k + 1, :]
        block = jnp.right_shift(p, shift)
        local = jnp.left_shift(jnp.right_shift(block, rshift), shift) + jnp.bitwise_and(p, nb - 1)
        local = jnp.where(jnp.bitwise_and(block, R - 1) == r, local, -1)
        wide = jnp.broadcast_to(local, (nb, nb))
        tall = wide.astype(F32).T
        for t in range(height // nb):
            spots = slice(t * nb, (t + 1) * nb)
            sel[spots, k * nb:(k + 1) * nb] = jnp.where(wide == sub + t * nb, 1.0, 0.0).astype(BF16)
            sel_t[k * nb:(k + 1) * nb, spots] = jnp.where(
                tall == (lane + t * nb).astype(F32), 1.0, 0.0).astype(BF16)

    load.wait()
    load_linv.wait()
    pl.semaphore_wait(barrier, R + jnp.minimum(c // 2, 1) + jnp.minimum((C - 1 - c) // 2, 1))

    def remote(src, dst, send, recv, where):
        return pltpu.make_async_remote_copy(
            src_ref=src, dst_ref=dst, send_sem=send, recv_sem=recv, device_id=where, device_id_type=MESH)

    def row_peer(off):
        return {"row": lax.rem(r + off, R)}

    def tp_copy(off):
        q = jnp.minimum(r, 1)
        return remote(a_v.at[0:nb, 0:nb], tp.at[pl.ds(pl.multiple_of(q * nb, nb), nb)],
                      tp_s.at[off - 1], tp_r.at[q], row_peer(off))

    def tops_copy(off):
        q = jnp.minimum(r, 1)
        return remote(a_v.at[0:nb], tops.at[pl.ds(pl.multiple_of(q * nb, nb), nb)],
                      to_s.at[off - 1], to_r.at[q], row_peer(off))

    def d_copy(off):
        return remote(dpart, dbuf.at[off - 1], d_s.at[off - 1], d_r.at[off - 1], row_peer(off))

    def rs_copy(off):
        to = lax.rem(r + off, R)
        return remote(pm.at[pl.ds(pl.multiple_of(to * ch, ch), ch)], rsbuf.at[off - 1],
                      rs_s.at[off - 1], rs_r.at[off - 1], {"row": to})

    def ag_copy(off):
        mine = pf.at[pl.ds(pl.multiple_of(r * ch, ch), ch)]
        return remote(mine, mine, ag_s.at[off - 1], ag_r.at[off - 1], row_peer(off))

    def ag_in(off):
        src = lax.rem(r - off + R, R)
        there = pf.at[pl.ds(pl.multiple_of(src * ch, ch), ch)]
        return remote(there, there, ag_s.at[off - 1], ag_r.at[off - 1], row_peer(off))

    def piece(side, k):
        if k < CHUNKS:
            return pan.at[side, pl.ds(k * ck, ck)]
        return dh.at[side, pl.ds((k - CHUNKS) * nb, nb)]

    def chain_copy(k):
        part = piece(s, k)
        return remote(part, part, ch_s.at[k], ch_r.at[k], {"col": jnp.minimum(c + 2, C - 2 + s)})

    def sib_copy(k):
        part = piece(s, k)
        return remote(part, part, sb_s.at[k], sb_r.at[k], sibling)

    def sib_in(k):
        part = piece(1 - s, k)
        return remote(part, part, sb_s.at[k], sb_r.at[k], sibling)

    is_top = r < 2
    at_root = c < 2

    @pl.when(at_root)
    def _():
        @pl.when(is_top)
        def _():
            for off in range(1, R):
                tp_copy(off).start()
            tp[pl.ds(pl.multiple_of(jnp.minimum(r, 1) * nb, nb), nb), :] = a_v[0:nb, 0:nb]

        dpart[...] = select(sel_t[...], a_v[:, 0:nb])
        for off in range(1, R):
            d_copy(off).start()

    ones = jnp.full((two, nb), 1.0, BF16)

    @pl.loop(0, TILES)
    def _(t):
        spots = pl.ds(pl.multiple_of(t * (height // TILES), height // TILES), height // TILES)
        hit[spots, :] = mm(sel[spots, :], ones)

    def panel(first, last):
        high, middle, low = thirds(tp[...])
        for k in range(first, last):
            spots = slice(k * ck, (k + 1) * ck)
            chosen = sel[spots, :]
            placed = mm(chosen, high) + (mm(chosen, middle) + mm(chosen, low))
            pan[s, spots, :] = jnp.where(hit[spots, :] > 0.5, placed, a_v[spots, 0:nb])
            chain_copy(k).start()
            sib_copy(k).start()

    @pl.when(at_root)
    def _():
        for q in range(2):
            @pl.when(r != q)
            def _():
                part = tp.at[q * nb:(q + 1) * nb]
                remote(part, part, tp_s.at[0], tp_r.at[q], row_peer(1)).wait_recv()
        panel(0, EARLY)

    @pl.loop(0, width // nb)
    def _(t):
        spots = pl.ds(pl.multiple_of(t * nb, nb), nb)
        pm[:, spots] = select(sel_t[...], a_v[:, spots])

    for off in range(1, R):
        rs_copy(off).start()

    @pl.when(is_top)
    def _():
        for off in range(1, R):
            tops_copy(off).start()
        tops[pl.ds(pl.multiple_of(jnp.minimum(r, 1) * nb, nb), nb), :] = a_v[0:nb, :]

    @pl.when(at_root)
    def _():
        total = dpart[...]
        for off in range(1, R):
            d_copy(off).wait_recv()
            total = total + dbuf[off - 1]
        dh[s] = total
        for k in range(CHUNKS, CHUNKS + 2):
            chain_copy(k).start()
            sib_copy(k).start()
        panel(EARLY, CHUNKS)

    def forward(k):
        @pl.when(c >= 2)
        def _():
            chain_copy(k).wait_recv()

            @pl.when(c + 2 < C)
            def _():
                chain_copy(k).start()
            sib_copy(k).start()

    for k in range(EARLY):
        forward(k)
    forward(CHUNKS)
    forward(CHUNKS + 1)

    own = pl.ds(pl.multiple_of(r * ch, ch), ch)
    total = pm[own, :]
    for off in range(1, R):
        rs_copy(off).wait_recv()
        total = total + rsbuf[off - 1]
    pf[own, :] = total
    for off in range(1, R):
        ag_copy(off).start()

    left = list(range(EARLY, CHUNKS))

    def some(count):
        for _ in range(min(count, len(left))):
            forward(left.pop(0))

    sib_in(CHUNKS).wait_recv()
    sib_in(CHUNKS + 1).wait_recv()
    upper00 = jnp.where(sub <= lane, exact(linv_ref[0], dh[0, 0:nb, :]), 0.0)
    res[0] = upper_inverse(upper00, sub, lane)
    some(1)
    res[1] = exact(dh[0, nb:two, :], res[0])
    upper01 = exact(linv_ref[0], dh[1, 0:nb, :])
    rest = dh[1, nb:two, :] - exact(res[1], upper01)
    upper11 = jnp.where(sub <= lane, exact(linv_ref[1], rest), 0.0)
    res[2] = -exact(res[0], upper01)
    some(1)
    res[3] = upper_inverse(upper11, sub, lane)
    some(2)
    res[2] = exact(res[2], res[3])
    mixed = -exact(exact(linv_ref[1], res[1]), linv_ref[0])
    some(1)

    for q in range(2):
        @pl.when(r != q)
        def _():
            part = tops.at[q * nb:(q + 1) * nb]
            remote(part, part, to_s.at[0], to_r.at[q], row_peer(1)).wait_recv()

    for t in range(width // nb):
        spots = slice(t * nb, (t + 1) * nb)
        placed = select(sel[...], tops[:, spots])
        asw[:, spots] = jnp.where(hit[...] > 0.5, placed, a_v[:, spots])
        some(1)

    for off in range(1, R):
        ag_in(off).wait_recv()

    inv_low0 = linv_ref[0]
    inv_low1 = linv_ref[1]
    u_f[0:nb, :] = dot3(halves(inv_low0), halves(pf[0:nb, :]))
    u_f[nb:two, :] = (dot3(halves(mixed), halves(pf[0:nb, :]))
                      + dot3(halves(inv_low1), halves(pf[nb:two, :])))
    high, low = halves(u_f[...])
    u_hi[...] = high
    u_lo[...] = low

    step = height // TILES
    inv0 = halves(res[0])
    cross = halves(res[2])
    inv1 = halves(res[3])

    def update(t, start):
        spots = pl.ds(start, step)
        left0 = halves(pan[0, spots, :])
        left1 = halves(pan[1, spots, :])
        low0 = dot3(left0, inv0)
        low1 = dot3(left0, cross) + dot3(left1, inv1)
        high, low = halves(jnp.concatenate([low0, low1], axis=1))
        asw[spots, :] = asw[spots, :] - dot3((high, low), (u_hi[...], u_lo[...]))

        @pl.when(c == 0)
        def _():
            asw[spots, 0:nb] = low0

        @pl.when(c == 1)
        def _():
            asw[spots, 0:nb] = low1

    per_tile = CHUNKS // TILES
    for t in range(TILES):
        some(1)
        while left and left[0] < (t + 1) * per_tile:
            some(1)
        for k in range(t * per_tile, (t + 1) * per_tile):
            sib_in(k).wait_recv()
        update(t, t * step)
        if t == 0:
            @pl.when(r == 0)
            def _():
                asw[0:nb, :] = u_f[0:nb, :]

                @pl.when(c == 0)
                def _():
                    asw[0:nb, 0:nb] = jnp.where(sub <= lane, u_f[0:nb, 0:nb], 0.0)

            @pl.when(r == 1)
            def _():
                asw[0:nb, :] = u_f[nb:two, :]

                @pl.when(c == 0)
                def _():
                    asw[0:nb, 0:nb] = res[1]

                @pl.when(c == 1)
                def _():
                    asw[0:nb, 0:nb] = jnp.where(sub <= lane, u_f[nb:two, 0:nb], 0.0)

    for off in range(1, R):
        rs_copy(off).wait_send()
        ag_copy(off).wait_send()

    @pl.when(is_top)
    def _():
        for off in range(1, R):
            tops_copy(off).wait_send()

        @pl.when(at_root)
        def _():
            for off in range(1, R):
                tp_copy(off).wait_send()

    for k in range(CHUNKS + 2):
        sib_copy(k).wait_send()

        @pl.when(c + 2 < C)
        def _():
            chain_copy(k).wait_send()

    @pl.when(at_root)
    def _():
        for off in range(1, R):
            d_copy(off).wait_send()


def on_device(matrix, pivots, lower_inverse):
    R = lax.axis_size("row")
    C = lax.axis_size("col")
    height, width = matrix.shape
    nb = lower_inverse.shape[1]
    two = 2 * nb
    dma = pltpu.SemaphoreType.DMA
    vm = pltpu.VMEM
    return pl.pallas_call(
        functools.partial(kernel, R, C, nb),
        out_shape=jax.ShapeDtypeStruct((height, width), F32),
        in_specs=[pl.BlockSpec(memory_space=pl.ANY)] * 3,
        out_specs=pl.BlockSpec(memory_space=pltpu.VMEM),
        scratch_shapes=[
            vm((height, width), F32), vm((2, nb), jnp.int32), vm((2, nb, nb), F32),
            vm((height, two), BF16), vm((two, height), BF16),
            vm((two, width), F32), vm((two, width), F32),
            vm((R - 1, two // R, width), F32), vm((two, width), F32),
            vm((two, nb), F32), vm((two, nb), F32), vm((R - 1, two, nb), F32),
            vm((2, two, nb), F32), vm((2, height, nb), F32), vm((4, nb, nb), F32),
            vm((two, width), BF16), vm((two, width), BF16), vm((two, width), F32),
            vm((height, nb), F32),
            dma, dma, dma, dma((R - 1,)), dma((R - 1,)), dma((R - 1,)), dma((2,)),
            dma((R - 1,)), dma((R - 1,)), dma((R - 1,)), dma((R - 1,)),
            dma((R - 1,)), dma((2,)), dma((CHUNKS + 2,)), dma((CHUNKS + 2,)),
            dma((CHUNKS + 2,)), dma((CHUNKS + 2,)),
        ],
        compiler_params=pltpu.CompilerParams(
            collective_id=0, has_side_effects=True, vmem_limit_bytes=56 * 1024 * 1024),
    )(matrix, pivots, lower_inverse)


def solution(mesh):
    return jax.shard_map(
        on_device,
        mesh=mesh,
        in_specs=(P("row", "col"), P(), P()),
        out_specs=P("row", "col"),
        check_vma=False,
    )
```

```python
import functools

import jax
import jax.numpy as jnp
from jax import lax
from jax.experimental import pallas as pl
from jax.experimental.pallas import tpu as pltpu
from jax.sharding import PartitionSpec as P

MESH = pl.DeviceIdType.MESH
F32 = jnp.float32
BF16 = jnp.bfloat16
CHUNKS = 16
EARLY = 3
TILES = 4


def mm(left, right):
    return jnp.dot(left, right, preferred_element_type=F32)


def exact(left, right):
    return jnp.dot(left, right, precision=lax.Precision.HIGHEST, preferred_element_type=F32)


def halves(value):
    high = value.astype(BF16)
    return high, (value - high.astype(F32)).astype(BF16)


def thirds(value):
    high = value.astype(BF16)
    rest = value - high.astype(F32)
    middle = rest.astype(BF16)
    return high, middle, (rest - middle.astype(F32)).astype(BF16)


def select(chosen, value):
    high, middle, low = thirds(value)
    return mm(chosen, high) + (mm(chosen, middle) + mm(chosen, low))


def dot3(left, right):
    left_high, left_low = left
    right_high, right_low = right
    return mm(left_high, right_high) + (mm(left_low, right_high) + mm(left_high, right_low))


def upper_inverse(upper, rows, cols):
    on_diag = rows == cols
    eye = jnp.where(on_diag, 1.0, 0.0)
    kept = jnp.where(on_diag, upper, 0.0)
    scaled = upper / jnp.sum(kept, axis=1, keepdims=True)
    power = jnp.where(rows < cols, -scaled, 0.0)
    result = eye + power
    reach = 2
    while reach < upper.shape[0]:
        power = exact(power, power)
        result = result + exact(result, power)
        reach = reach * 2
    return result / jnp.sum(kept, axis=0, keepdims=True)


def kernel(R, C, nb, a_hbm, piv_hbm, linv_hbm, asw,
           a_v, piv_ref, linv_ref, sel, sel_t, pm, pf, rsbuf, tops, tp, dpart, dbuf, dh, pan, res,
           u_hi, u_lo, u_f, hit,
           load_sem, piv_sem, linv_sem, d_s, d_r, tp_s, tp_r, rs_s, rs_r, ag_s, ag_r,
           to_s, to_r, ch_s, ch_r, sb_s, sb_r):
    height, width = a_v.shape
    two = 2 * nb
    ch = two // R
    ck = height // CHUNKS
    r = lax.axis_index("row")
    c = lax.axis_index("col")
    s = lax.rem(c, 2)
    sibling = {"col": c + 1 - 2 * s}

    load = pltpu.make_async_copy(a_hbm, a_v, load_sem)
    load_piv = pltpu.make_async_copy(piv_hbm, piv_ref, piv_sem)
    load_linv = pltpu.make_async_copy(linv_hbm, linv_ref, linv_sem)
    load_piv.start()
    load.start()
    load_linv.start()

    barrier = pltpu.get_barrier_semaphore()
    for off in range(1, R):
        pl.semaphore_signal(barrier, inc=1, device_id={"row": lax.rem(r + off, R)}, device_id_type=MESH)
    has_after = c + 2 < C
    has_before = c >= 2

    @pl.when(has_after)
    def _():
        pl.semaphore_signal(barrier, inc=1, device_id={"col": jnp.minimum(c + 2, C - 1)}, device_id_type=MESH)

    @pl.when(has_before)
    def _():
        pl.semaphore_signal(barrier, inc=1, device_id={"col": jnp.maximum(c - 2, 0)}, device_id_type=MESH)

    pl.semaphore_signal(barrier, inc=1, device_id=sibling, device_id_type=MESH)

    load_piv.wait()
    shift = nb.bit_length() - 1
    rshift = R.bit_length() - 1
    lane = lax.broadcasted_iota(jnp.int32, (nb, nb), 1)
    sub = lax.broadcasted_iota(jnp.int32, (nb, nb), 0)
    for k in range(2):
        p = piv_ref[k:k + 1, :]
        block = jnp.right_shift(p, shift)
        local = jnp.left_shift(jnp.right_shift(block, rshift), shift) + jnp.bitwise_and(p, nb - 1)
        local = jnp.where(jnp.bitwise_and(block, R - 1) == r, local, -1)
        wide = jnp.broadcast_to(local, (nb, nb))
        tall = wide.astype(F32).T
        for t in range(height // nb):
            spots = slice(t * nb, (t + 1) * nb)
            sel[spots, k * nb:(k + 1) * nb] = jnp.where(wide == sub + t * nb, 1.0, 0.0).astype(BF16)
            sel_t[k * nb:(k + 1) * nb, spots] = jnp.where(
                tall == (lane + t * nb).astype(F32), 1.0, 0.0).astype(BF16)

    load.wait()
    load_linv.wait()
    pl.semaphore_wait(barrier, R + jnp.minimum(c // 2, 1) + jnp.minimum((C - 1 - c) // 2, 1))

    def remote(src, dst, send, recv, where):
        return pltpu.make_async_remote_copy(
            src_ref=src, dst_ref=dst, send_sem=send, recv_sem=recv, device_id=where, device_id_type=MESH)

    def row_peer(off):
        return {"row": lax.rem(r + off, R)}

    def tp_copy(off):
        q = jnp.minimum(r, 1)
        return remote(a_v.at[0:nb, 0:nb], tp.at[pl.ds(pl.multiple_of(q * nb, nb), nb)],
                      tp_s.at[off - 1], tp_r.at[q], row_peer(off))

    def tops_copy(off):
        q = jnp.minimum(r, 1)
        return remote(a_v.at[0:nb], tops.at[pl.ds(pl.multiple_of(q * nb, nb), nb)],
                      to_s.at[off - 1], to_r.at[q], row_peer(off))

    def d_copy(off):
        return remote(dpart, dbuf.at[off - 1], d_s.at[off - 1], d_r.at[off - 1], row_peer(off))

    def rs_copy(off):
        to = lax.rem(r + off, R)
        return remote(pm.at[pl.ds(pl.multiple_of(to * ch, ch), ch)], rsbuf.at[off - 1],
                      rs_s.at[off - 1], rs_r.at[off - 1], {"row": to})

    def ag_copy(off):
        mine = pf.at[pl.ds(pl.multiple_of(r * ch, ch), ch)]
        return remote(mine, mine, ag_s.at[off - 1], ag_r.at[off - 1], row_peer(off))

    def ag_in(off):
        src = lax.rem(r - off + R, R)
        there = pf.at[pl.ds(pl.multiple_of(src * ch, ch), ch)]
        return remote(there, there, ag_s.at[off - 1], ag_r.at[off - 1], row_peer(off))

    def piece(side, k):
        if k < CHUNKS:
            return pan.at[side, pl.ds(k * ck, ck)]
        return dh.at[side, pl.ds((k - CHUNKS) * nb, nb)]

    def chain_copy(k):
        part = piece(s, k)
        return remote(part, part, ch_s.at[k], ch_r.at[k], {"col": jnp.minimum(c + 2, C - 2 + s)})

    def sib_copy(k):
        part = piece(s, k)
        return remote(part, part, sb_s.at[k], sb_r.at[k], sibling)

    def sib_in(k):
        part = piece(1 - s, k)
        return remote(part, part, sb_s.at[k], sb_r.at[k], sibling)

    is_top = r < 2
    at_root = c < 2

    @pl.when(at_root)
    def _():
        @pl.when(is_top)
        def _():
            for off in range(1, R):
                tp_copy(off).start()
            tp[pl.ds(pl.multiple_of(jnp.minimum(r, 1) * nb, nb), nb), :] = a_v[0:nb, 0:nb]

        dpart[...] = select(sel_t[...], a_v[:, 0:nb])
        for off in range(1, R):
            d_copy(off).start()

    ones = jnp.full((two, nb), 1.0, BF16)

    @pl.loop(0, TILES)
    def _(t):
        spots = pl.ds(pl.multiple_of(t * (height // TILES), height // TILES), height // TILES)
        hit[spots, :] = mm(sel[spots, :], ones)

    def panel(first, last):
        high, middle, low = thirds(tp[...])
        for k in range(first, last):
            spots = slice(k * ck, (k + 1) * ck)
            chosen = sel[spots, :]
            placed = mm(chosen, high) + (mm(chosen, middle) + mm(chosen, low))
            pan[s, spots, :] = jnp.where(hit[spots, :] > 0.5, placed, a_v[spots, 0:nb])
            chain_copy(k).start()
            sib_copy(k).start()

    @pl.loop(0, width // nb)
    def _(t):
        spots = pl.ds(pl.multiple_of(t * nb, nb), nb)
        pm[:, spots] = select(sel_t[...], a_v[:, spots])

    @pl.when(at_root)
    def _():
        for q in range(2):
            @pl.when(r != q)
            def _():
                part = tp.at[q * nb:(q + 1) * nb]
                remote(part, part, tp_s.at[0], tp_r.at[q], row_peer(1)).wait_recv()
        panel(0, EARLY)

    for off in range(1, R):
        rs_copy(off).start()

    @pl.when(is_top)
    def _():
        for off in range(1, R):
            tops_copy(off).start()
        tops[pl.ds(pl.multiple_of(jnp.minimum(r, 1) * nb, nb), nb), :] = a_v[0:nb, :]

    @pl.when(at_root)
    def _():
        total = dpart[...]
        for off in range(1, R):
            d_copy(off).wait_recv()
            total = total + dbuf[off - 1]
        dh[s] = total
        for k in range(CHUNKS, CHUNKS + 2):
            chain_copy(k).start()
            sib_copy(k).start()
        panel(EARLY, CHUNKS)

    def forward(k):
        @pl.when(c >= 2)
        def _():
            chain_copy(k).wait_recv()

            @pl.when(c + 2 < C)
            def _():
                chain_copy(k).start()
            sib_copy(k).start()

    for k in range(EARLY):
        forward(k)
    forward(CHUNKS)
    forward(CHUNKS + 1)

    own = pl.ds(pl.multiple_of(r * ch, ch), ch)
    total = pm[own, :]
    for off in range(1, R):
        rs_copy(off).wait_recv()
        total = total + rsbuf[off - 1]
    pf[own, :] = total
    for off in range(1, R):
        ag_copy(off).start()

    left = list(range(EARLY, CHUNKS))

    def some(count):
        for _ in range(min(count, len(left))):
            forward(left.pop(0))

    sib_in(CHUNKS).wait_recv()
    sib_in(CHUNKS + 1).wait_recv()
    upper00 = jnp.where(sub <= lane, exact(linv_ref[0], dh[0, 0:nb, :]), 0.0)
    res[0] = upper_inverse(upper00, sub, lane)
    some(1)
    res[1] = exact(dh[0, nb:two, :], res[0])
    upper01 = exact(linv_ref[0], dh[1, 0:nb, :])
    rest = dh[1, nb:two, :] - exact(res[1], upper01)
    upper11 = jnp.where(sub <= lane, exact(linv_ref[1], rest), 0.0)
    res[2] = -exact(res[0], upper01)
    some(1)
    res[3] = upper_inverse(upper11, sub, lane)
    some(2)
    res[2] = exact(res[2], res[3])
    mixed = -exact(exact(linv_ref[1], res[1]), linv_ref[0])
    some(1)

    for q in range(2):
        @pl.when(r != q)
        def _():
            part = tops.at[q * nb:(q + 1) * nb]
            remote(part, part, to_s.at[0], to_r.at[q], row_peer(1)).wait_recv()

    for t in range(width // nb):
        spots = slice(t * nb, (t + 1) * nb)
        placed = select(sel[...], tops[:, spots])
        asw[:, spots] = jnp.where(hit[...] > 0.5, placed, a_v[:, spots])
        some(1)

    for off in range(1, R):
        ag_in(off).wait_recv()

    inv_low0 = linv_ref[0]
    inv_low1 = linv_ref[1]
    u_f[0:nb, :] = dot3(halves(inv_low0), halves(pf[0:nb, :]))
    u_f[nb:two, :] = (dot3(halves(mixed), halves(pf[0:nb, :]))
                      + dot3(halves(inv_low1), halves(pf[nb:two, :])))
    high, low = halves(u_f[...])
    u_hi[...] = high
    u_lo[...] = low

    step = height // TILES
    inv0 = halves(res[0])
    cross = halves(res[2])
    inv1 = halves(res[3])

    def update(t, start):
        spots = pl.ds(start, step)
        left0 = halves(pan[0, spots, :])
        left1 = halves(pan[1, spots, :])
        low0 = dot3(left0, inv0)
        low1 = dot3(left0, cross) + dot3(left1, inv1)
        high, low = halves(jnp.concatenate([low0, low1], axis=1))
        asw[spots, :] = asw[spots, :] - dot3((high, low), (u_hi[...], u_lo[...]))

        @pl.when(c == 0)
        def _():
            asw[spots, 0:nb] = low0

        @pl.when(c == 1)
        def _():
            asw[spots, 0:nb] = low1

    per_tile = CHUNKS // TILES
    for t in range(TILES):
        some(1)
        while left and left[0] < (t + 1) * per_tile:
            some(1)
        for k in range(t * per_tile, (t + 1) * per_tile):
            sib_in(k).wait_recv()
        update(t, t * step)
        if t == 0:
            @pl.when(r == 0)
            def _():
                asw[0:nb, :] = u_f[0:nb, :]

                @pl.when(c == 0)
                def _():
                    asw[0:nb, 0:nb] = jnp.where(sub <= lane, u_f[0:nb, 0:nb], 0.0)

            @pl.when(r == 1)
            def _():
                asw[0:nb, :] = u_f[nb:two, :]

                @pl.when(c == 0)
                def _():
                    asw[0:nb, 0:nb] = res[1]

                @pl.when(c == 1)
                def _():
                    asw[0:nb, 0:nb] = jnp.where(sub <= lane, u_f[nb:two, 0:nb], 0.0)

    for off in range(1, R):
        rs_copy(off).wait_send()
        ag_copy(off).wait_send()

    @pl.when(is_top)
    def _():
        for off in range(1, R):
            tops_copy(off).wait_send()

        @pl.when(at_root)
        def _():
            for off in range(1, R):
                tp_copy(off).wait_send()

    for k in range(CHUNKS + 2):
        sib_copy(k).wait_send()

        @pl.when(c + 2 < C)
        def _():
            chain_copy(k).wait_send()

    @pl.when(at_root)
    def _():
        for off in range(1, R):
            d_copy(off).wait_send()


def on_device(matrix, pivots, lower_inverse):
    R = lax.axis_size("row")
    C = lax.axis_size("col")
    height, width = matrix.shape
    nb = lower_inverse.shape[1]
    two = 2 * nb
    dma = pltpu.SemaphoreType.DMA
    vm = pltpu.VMEM
    return pl.pallas_call(
        functools.partial(kernel, R, C, nb),
        out_shape=jax.ShapeDtypeStruct((height, width), F32),
        in_specs=[pl.BlockSpec(memory_space=pl.ANY)] * 3,
        out_specs=pl.BlockSpec(memory_space=pltpu.VMEM),
        scratch_shapes=[
            vm((height, width), F32), vm((2, nb), jnp.int32), vm((2, nb, nb), F32),
            vm((height, two), BF16), vm((two, height), BF16),
            vm((two, width), F32), vm((two, width), F32),
            vm((R - 1, two // R, width), F32), vm((two, width), F32),
            vm((two, nb), F32), vm((two, nb), F32), vm((R - 1, two, nb), F32),
            vm((2, two, nb), F32), vm((2, height, nb), F32), vm((4, nb, nb), F32),
            vm((two, width), BF16), vm((two, width), BF16), vm((two, width), F32),
            vm((height, nb), F32),
            dma, dma, dma, dma((R - 1,)), dma((R - 1,)), dma((R - 1,)), dma((2,)),
            dma((R - 1,)), dma((R - 1,)), dma((R - 1,)), dma((R - 1,)),
            dma((R - 1,)), dma((2,)), dma((CHUNKS + 2,)), dma((CHUNKS + 2,)),
            dma((CHUNKS + 2,)), dma((CHUNKS + 2,)),
        ],
        compiler_params=pltpu.CompilerParams(
            collective_id=0, has_side_effects=True, vmem_limit_bytes=56 * 1024 * 1024),
    )(matrix, pivots, lower_inverse)


def solution(mesh):
    return jax.shard_map(
        on_device,
        mesh=mesh,
        in_specs=(P("row", "col"), P(), P()),
        out_specs=P("row", "col"),
        check_vma=False,
    )
```
